1024 devices in a mesh: node: 128 (over z_lo, y, core), dev: 8 (over x, z_hi).
Axes of the slice: x: 4, y: 8, z: 16 (z_hi: 2, z_lo: 8; z = z_hi * 8 + z_lo), core: 2. Of those that a mesh axis runs over, the one named last changes fastest.
Arguments:
- coarse_state: float32 [5, 2048, 2048], P(None, 'node', 'dev'), as said below
- fine_state: float32 [6144, 5, 512], P(('node', 'dev')), as said below
- fine_anchor: int32 [1024, 2, 3], P(('node', 'dev')), may hold values from 2 to 10, as said below
- fine_owner: int32 [1024, 2, 2], P(('node', 'dev')), may hold values from 0 to 5, as said below
Outputs:
- coarse_new: float32 [5, 2048, 2048], P(None, 'node', 'dev')
- fine_new: float32 [6144, 5, 512], P(('node', 'dev'))
The draws below stay inside these ranges and needn't reach their ends.
Inputs may be any that keep to these rules, and one draw needn't show every extreme that they name: `coarse_state`: density in [0.5, 2], every velocity component in [-0.3, 0.3], pressure in [0.5, 2] in every cell, with E = p / 0.4 + rho |u|^2 / 2. `fine_state`: same law as coarse_state in every slot; slots that hold no fine box are not read. `fine_anchor`: z and y anchors lie in [2, 10]; the x anchor of fine box 0 lies in [2, 3], that of fine box 1 in [10, 10]. Fine regions lie 2 or more coarse cells inside their box and never touch each other. `fine_owner`: k < 4 and s < 6; no two fine boxes share a slot of a device; every device holds at most 6 fine boxes and in every draw some devices hold exactly 6, while the mean is 2; both fine boxes of one coarse box may have the same k.
All inputs are finite; a program needn't handle non-finite values.
Results may differ from the reference program's by a relative error of at most 0.0003.
Values sent between devices are 32-bit elements; how exact they have to be, the bound alone decides.
No kernel may reach another device: no remote copies, remote signals or barrier semaphores. Data moves between devices by JAX's collectives and lax.ppermute only.
A program may use at most 64 MiB of HBM per device.

```python
import jax
import jax.numpy as jnp
from jax import lax

B = 16
F = 8
R = 4
FPC = 2
SPAN = 4
CAP = 6
NZ = 2048
NXY = 2048
SLOTS = 6144
N_NODE = 128
N_DEV = 8
DEVICES = 1024


def assemble(density, velocity_x, velocity_y, velocity_z, pressure):
    kinetic = 0.5 * density * (velocity_x * velocity_x + velocity_y * velocity_y + velocity_z * velocity_z)
    return jnp.stack([density, density * velocity_x, density * velocity_y, density * velocity_z, pressure / 0.4 + kinetic])


def draw_coarse_state(key, part):
    key = jax.random.fold_in(key, 11)
    subkeys = jax.random.split(key, 5)
    field_shape = (NZ, NXY)
    density = jax.random.uniform(subkeys[0], field_shape, minval=0.5, maxval=2.0)
    pressure = jax.random.uniform(subkeys[1], field_shape, minval=0.5, maxval=2.0)
    velocity_x = jax.random.uniform(subkeys[2], field_shape, minval=-0.3, maxval=0.3)
    velocity_y = jax.random.uniform(subkeys[3], field_shape, minval=-0.3, maxval=0.3)
    velocity_z = jax.random.uniform(subkeys[4], field_shape, minval=-0.3, maxval=0.3)
    return assemble(density, velocity_x, velocity_y, velocity_z, pressure)


def draw_fine_state(key, part):
    key = jax.random.fold_in(key, 17)
    subkeys = jax.random.split(key, 5)
    field_shape = (SLOTS, F * F * F)
    density = jax.random.uniform(subkeys[0], field_shape, minval=0.5, maxval=2.0)
    pressure = jax.random.uniform(subkeys[1], field_shape, minval=0.5, maxval=2.0)
    velocity_x = jax.random.uniform(subkeys[2], field_shape, minval=-0.3, maxval=0.3)
    velocity_y = jax.random.uniform(subkeys[3], field_shape, minval=-0.3, maxval=0.3)
    velocity_z = jax.random.uniform(subkeys[4], field_shape, minval=-0.3, maxval=0.3)
    return jnp.moveaxis(assemble(density, velocity_x, velocity_y, velocity_z, pressure), 0, 1)


def draw_fine_anchor(key, part):
    key = jax.random.fold_in(key, 23)
    subkeys = jax.random.split(key, 4)
    depth = jax.random.randint(subkeys[0], (DEVICES, FPC, 1), 2, B - R - 1)
    across = jax.random.randint(subkeys[1], (DEVICES, FPC, 1), 2, B - R - 1)
    lower_x = jax.random.randint(subkeys[2], (DEVICES, 1, 1), 2, B // 2 - R)
    upper_x = jax.random.randint(subkeys[3], (DEVICES, 1, 1), B // 2 + 2, B - R - 1)
    along_x = jnp.concatenate([lower_x, upper_x], axis=1)
    return jnp.concatenate([depth, along_x, across], axis=2).astype(jnp.int32)


def shuffle_slots(draw_seed):
    return jax.random.permutation(draw_seed, CAP)


def draw_fine_owner(key, part):
    key = jax.random.fold_in(key, 37)
    subkeys = jax.random.split(key, 5)
    groups = N_NODE // SPAN
    rotate = jax.random.randint(subkeys[0], (1, N_DEV), 0, SPAN)
    node_ids = jnp.arange(N_NODE, dtype=jnp.int32)[:, None]
    shifted = (node_ids - rotate) % N_NODE
    position = shifted % SPAN
    group_ids = shifted // SPAN
    spare = jax.random.randint(subkeys[1], (groups, N_DEV), 0, SPAN - 1)
    spare_here = jnp.take_along_axis(spare, group_ids, axis=0)
    flips = jax.random.randint(subkeys[2], (groups, N_DEV), 0, FPC)
    flip_here = jnp.take_along_axis(flips, group_ids, axis=0)
    reach = jax.random.randint(subkeys[3], (N_NODE, N_DEV, FPC), 0, (SPAN - 1 - spare_here)[..., None])
    seeds = jax.random.split(subkeys[4], groups * N_DEV)
    orders = jax.vmap(shuffle_slots)(seeds).reshape(groups, N_DEV, CAP)
    order_here = jnp.take_along_axis(orders, jnp.broadcast_to(group_ids[..., None], (N_NODE, N_DEV, CAP)), axis=0)
    is_spare = (position == spare_here)[..., None]
    rank = position - (position > spare_here).astype(jnp.int32)
    member_ids = jnp.arange(FPC, dtype=jnp.int32)[None, None, :]
    heavy_slot = jnp.take_along_axis(order_here, rank[..., None] * FPC + member_ids, axis=2)
    spare_slot = (member_ids + flip_here[..., None]) % FPC
    offset = jnp.where(is_spare, reach, jnp.broadcast_to((SPAN - 1 - position)[..., None], (N_NODE, N_DEV, FPC)))
    slot_ids = jnp.where(is_spare, spare_slot, heavy_slot)
    return jnp.stack([offset, slot_ids], axis=-1).reshape(DEVICES, FPC, 2).astype(jnp.int32)


def setup_inputs(seed: int = 0) -> dict:
    key_list = jax.random.split(jax.random.key(seed), 5)
    coarse_state = draw_coarse_state(jax.random.fold_in(key_list[4], 71), 0)
    fine_state = draw_fine_state(jax.random.fold_in(key_list[4], 71), 0)
    fine_anchor = draw_fine_anchor(jax.random.fold_in(key_list[4], 71), 0)
    fine_owner = draw_fine_owner(jax.random.fold_in(key_list[4], 71), 0)
    return {"coarse_state": coarse_state, "fine_state": fine_state, "fine_anchor": fine_anchor, "fine_owner": fine_owner}


GAMMA = 1.4
RATIO = 0.06

def primitives(conserved, member):
    density = conserved[0]
    velocity = conserved[member] / density
    kinetic = 0.5 * (conserved[1] * conserved[1] + conserved[2] * conserved[2] + conserved[3] * conserved[3]) / density
    pressure = (GAMMA - 1.0) * (conserved[4] - kinetic)
    sound_speed = jnp.sqrt(GAMMA * pressure / density)
    return (velocity, pressure, sound_speed)

def physical(conserved, velocity, pressure, member):
    pieces = []
    for position in range(5):
        entry_term = conserved[position] * velocity
        if position == member:
            entry_term = entry_term + pressure
        if position == 4:
            entry_term = entry_term + pressure * velocity
        pieces.append(entry_term)
    return jnp.stack(pieces)

def rusanov(lower_cells, upper_cells, member):
    velocity_low, pressure_low, sound_low = primitives(lower_cells, member)
    velocity_up, pressure_up, sound_up = primitives(upper_cells, member)
    wave_speed = jnp.maximum(jnp.abs(velocity_low) + sound_low, jnp.abs(velocity_up) + sound_up)
    average = 0.5 * (physical(lower_cells, velocity_low, pressure_low, member) + physical(upper_cells, velocity_up, pressure_up, member))
    return average - 0.5 * wave_speed * (upper_cells - lower_cells)

def advance(padded):
    interior = padded[:, 1:-1, 1:-1, 1:-1]
    flux_z = rusanov(padded[:, :-1, 1:-1, 1:-1], padded[:, 1:, 1:-1, 1:-1], 3)
    flux_x = rusanov(padded[:, 1:-1, :-1, 1:-1], padded[:, 1:-1, 1:, 1:-1], 1)
    flux_y = rusanov(padded[:, 1:-1, 1:-1, :-1], padded[:, 1:-1, 1:-1, 1:], 2)
    change = flux_z[:, 1:] - flux_z[:, :-1] + (flux_x[:, :, 1:] - flux_x[:, :, :-1]) + (flux_y[:, :, :, 1:] - flux_y[:, :, :, :-1])
    return (interior - RATIO * change, flux_z, flux_x, flux_y)

def minmod(lower_diff, upper_diff):
    smaller = jnp.where(jnp.abs(lower_diff) < jnp.abs(upper_diff), lower_diff, upper_diff)
    return jnp.where(lower_diff * upper_diff > 0.0, smaller, 0.0)

def interpolate(block):
    center = block[:, 1:-1, 1:-1, 1:-1]
    slope_z = minmod(center - block[:, :-2, 1:-1, 1:-1], block[:, 2:, 1:-1, 1:-1] - center)
    slope_x = minmod(center - block[:, 1:-1, :-2, 1:-1], block[:, 1:-1, 2:, 1:-1] - center)
    slope_y = minmod(center - block[:, 1:-1, 1:-1, :-2], block[:, 1:-1, 1:-1, 2:] - center)
    child_signs = jnp.array([-1.0, 1.0], jnp.float32)
    sign_z = child_signs.reshape(1, 1, 2, 1, 1, 1, 1)
    sign_x = child_signs.reshape(1, 1, 1, 1, 2, 1, 1)
    sign_y = child_signs.reshape(1, 1, 1, 1, 1, 1, 2)
    spread = center[:, :, None, :, None, :, None]
    slopes = slope_z[:, :, None, :, None, :, None] * sign_z + slope_x[:, :, None, :, None, :, None] * sign_x + slope_y[:, :, None, :, None, :, None] * sign_y
    coarse_cells = center.shape[1]
    refined = (spread + 0.25 * slopes).reshape(5, 2 * coarse_cells, 2 * coarse_cells, 2 * coarse_cells)
    return refined[:, 1:-1, 1:-1, 1:-1]

def fine_steps(fine_box, old_block, new_block):
    face_sums = None
    for substep in range(2):
        if substep == 0:
            source = old_block
        else:
            source = 0.5 * (old_block + new_block)
        padded = interpolate(source).at[:, 1:-1, 1:-1, 1:-1].set(fine_box)
        fine_box, flux_z, flux_x, flux_y = advance(padded)
        boundary = jnp.stack([flux_z[:, 0], flux_z[:, -1], flux_x[:, :, 0], flux_x[:, :, -1], flux_y[:, :, :, 0], flux_y[:, :, :, -1]])
        face_sums = boundary if face_sums is None else face_sums + boundary
    region_edge = fine_box.shape[1] // 2
    registers = 0.125 * face_sums.reshape(6, 5, region_edge, 2, region_edge, 2).sum(axis=(3, 5))
    average = 0.125 * fine_box.reshape(5, region_edge, 2, region_edge, 2, region_edge, 2).sum(axis=(2, 4, 6))
    return (fine_box, average, registers)

def block_at(field, anchor, block_edge):
    start_zero = jnp.zeros((), jnp.int32)
    return lax.dynamic_slice(field, (start_zero, anchor[0] - 2, anchor[1] - 2, anchor[2] - 2), (5, block_edge, block_edge, block_edge))

def reflux_box(coarse_field, fluxes, anchor, registers, region_width):
    start_zero = jnp.zeros((), jnp.int32)
    for axis_pos in range(3):
        for face_side in range(2):
            face_start = [start_zero, anchor[0], anchor[1], anchor[2]]
            face_start[axis_pos + 1] = anchor[axis_pos] + face_side * region_width
            cell_start = list(face_start)
            cell_start[axis_pos + 1] = anchor[axis_pos] + (face_side * (region_width + 1) - 1)
            extent = [5, region_width, region_width, region_width]
            extent[axis_pos + 1] = 1
            coarse_face = lax.dynamic_slice(fluxes[axis_pos], face_start, extent)
            register = jnp.expand_dims(registers[2 * axis_pos + face_side], axis_pos + 1)
            outside_cells = lax.dynamic_slice(coarse_field, cell_start, extent)
            factor = RATIO * (1.0 - 2.0 * face_side)
            coarse_field = lax.dynamic_update_slice(coarse_field, outside_cells + factor * (coarse_face - register), cell_start)
    return coarse_field

def average_down(coarse_field, anchor, average):
    start_zero = jnp.zeros((), jnp.int32)
    return lax.dynamic_update_slice(coarse_field, average, (start_zero, anchor[0], anchor[1], anchor[2]))

def reference(coarse_state, fine_state, fine_anchor, fine_owner):
    coarse_grid = coarse_state.reshape(5, NZ, N_DEV * B, B)
    slot_boxes = fine_state.reshape(SLOTS, 5, F, F, F)
    block_edge = R + 4

    def per_box(box_index):
        node_pos = box_index // N_DEV
        dev_pos = box_index % N_DEV
        z_rows = (node_pos * B - 1 + jnp.arange(B + 2, dtype=jnp.int32)) % NZ
        x_rows = (dev_pos * B - 1 + jnp.arange(B + 2, dtype=jnp.int32)) % (N_DEV * B)
        padded = jnp.take(jnp.take(coarse_grid, z_rows, axis=1), x_rows, axis=2)
        padded = jnp.concatenate([padded[..., -1:], padded, padded[..., :1]], axis=3)
        stepped, flux_z, flux_x, flux_y = advance(padded)
        coarse_box = padded[:, 1:-1, 1:-1, 1:-1]
        anchors = fine_anchor[box_index]
        owners = fine_owner[box_index]
        results = []
        targets = []
        for member in range(FPC):
            old_block = block_at(coarse_box, anchors[member], block_edge)
            new_block = block_at(stepped, anchors[member], block_edge)
            target = ((node_pos + owners[member, 0]) % N_NODE * N_DEV + dev_pos) * CAP + owners[member, 1]
            fine_box = lax.dynamic_index_in_dim(slot_boxes, target, 0, keepdims=False)
            results.append(fine_steps(fine_box, old_block, new_block))
            targets.append(target.astype(jnp.int32))
        coarse_out = stepped
        for member in range(FPC):
            coarse_out = reflux_box(coarse_out, (flux_z, flux_x, flux_y), anchors[member], results[member][2], R)
        for member in range(FPC):
            coarse_out = average_down(coarse_out, anchors[member], results[member][1])
        return (coarse_out, jnp.stack([outcome[0] for outcome in results]), jnp.stack(targets))
    coarse_boxes, fine_results, targets = lax.map(per_box, jnp.arange(DEVICES, dtype=jnp.int32))
    coarse_new = coarse_boxes.reshape(N_NODE, N_DEV, 5, B, B, B).transpose(2, 0, 3, 1, 4, 5).reshape(5, NZ, NXY)
    fine_new = jnp.zeros((SLOTS, 5, F, F, F), jnp.float32).at[targets.reshape(-1)].set(fine_results.reshape(-1, 5, F, F, F))
    return (coarse_new, fine_new.reshape(SLOTS, 5, F * F * F))
```

```python
import functools

import jax
import jax.numpy as jnp
from jax import lax
from jax.experimental import pallas as pl
from jax.experimental.pallas import tpu as pltpu
from jax.sharding import PartitionSpec as P

B = 16
ROW = B * B
CAP = 6
SPAN = 4
SLOT_ROWS = 24
GAMMA = 1.4
RATIO = 0.06
VMEM = pltpu.VMEM
SMEM = pltpu.SMEM


def iota(shape, dim):
    return lax.broadcasted_iota(jnp.int32, shape, dim)


def roll(value, shift, axis):
    size = value.shape[axis]
    return pltpu.roll(value, shift % size, axis)


def take(value, index, axis):
    return jnp.take_along_axis(value, index, axis=axis, mode="promise_in_bounds")


def pack_kernel(coarse_ref, fine_ref, slots_ref, edges_ref):
    lane = iota((B, 128), 1)
    x_low = jnp.zeros((B, 128), jnp.float32)
    x_high = jnp.zeros((B, 128), jnp.float32)
    for c in range(5):
        here = (lane >= c * B) & (lane < (c + 1) * B)
        x_low = jnp.where(here, roll(coarse_ref[c, :, :128], c * B, 1), x_low)
        x_high = jnp.where(here, roll(coarse_ref[c, :, 128:], (c + 1) * B, 1), x_high)
    edges_ref[0] = x_low
    edges_ref[1] = x_high
    for slot in range(CAP):
        for c in range(5):
            for tile in range(4):
                at = slot * SLOT_ROWS + c * 4 + tile
                slots_ref[at : at + 1, :] = fine_ref[
                    c, slot : slot + 1, tile * 128 : (tile + 1) * 128
                ]
        at = slot * SLOT_ROWS + 20
        slots_ref[at : at + 4, :] = jnp.zeros((4, 128), jnp.float32)
        if slot < 5:
            slots_ref[at : at + 1, :] = coarse_ref[slot, 0:1, :128]
            slots_ref[at + 1 : at + 2, :] = coarse_ref[slot, 0:1, 128:]


def cell_terms(state):
    inverse = 1.0 / state[0]
    squares = state[1] * state[1] + state[2] * state[2] + state[3] * state[3]
    pressure = (GAMMA - 1.0) * (state[4] - 0.5 * squares * inverse)
    sound = jnp.sqrt(GAMMA * pressure * inverse)
    return inverse, pressure, sound


def face_flux(low, low_terms, up, up_terms, member):
    def side(state, terms):
        inverse, pressure, sound = terms
        velocity = state[member] * inverse
        flux = [entry * velocity for entry in state]
        flux[member] = flux[member] + pressure
        flux[4] = flux[4] + pressure * velocity
        return flux, jnp.abs(velocity) + sound

    flux_low, speed_low = side(low, low_terms)
    flux_up, speed_up = side(up, up_terms)
    half_speed = 0.5 * jnp.maximum(speed_low, speed_up)
    return [
        0.5 * (flux_low[c] + flux_up[c]) - half_speed * (up[c] - low[c]) for c in range(5)
    ]


def minmod(lower_diff, upper_diff):
    smaller = jnp.where(jnp.abs(lower_diff) < jnp.abs(upper_diff), lower_diff, upper_diff)
    return jnp.where(lower_diff * upper_diff > 0.0, smaller, 0.0)


def step_kernel(
    anchor_ref,
    owner_ref,
    coarse_ref,
    own_ref,
    one_ref,
    two_ref,
    three_ref,
    pair_ref,
    relay_ref,
    z_before_ref,
    out_ref,
    result_ref,
    half_ref,
    boxes_ref,
):
    z0 = [anchor_ref[0, j, 0] - 2 for j in range(2)]
    x0 = [anchor_ref[0, j, 1] - 2 for j in range(2)]
    y0 = [anchor_ref[0, j, 2] - 2 for j in range(2)]
    shifts = [x0[j] * B + y0[j] for j in range(2)]

    for j in range(2):
        for k, source in enumerate((own_ref, one_ref, two_ref, three_ref)):

            @pl.when(owner_ref[0, j, 0] == k)
            def _(j=j, source=source):
                boxes_ref[j] = source[owner_ref[0, j, 1]]

    odd = lax.rem(lax.axis_index("dev"), 2)
    from_relay = relay_ref[1 - odd]
    x_before = jnp.where(odd == 1, pair_ref[1], from_relay)
    x_after = jnp.where(odd == 1, from_relay, pair_ref[0])

    state = [coarse_ref[c] for c in range(5)]
    terms = cell_terms(state)
    big = (B, ROW)
    z_at, lane = iota(big, 0), iota(big, 1)
    x_at, y_at = lane >> 4, lane & (B - 1)

    def z_neighbour(c, up):
        if up:
            edge = jnp.concatenate([one_ref[c, 20:21, :], one_ref[c, 21:22, :]], axis=1)
            return jnp.where(z_at == B - 1, edge, roll(state[c], -1, 0))
        return jnp.where(z_at == 0, z_before_ref[c, B - 1 : B, :], roll(state[c], 1, 0))

    def x_neighbour(c, up):
        if up:
            edge = roll(x_after, -(c + 1) * B, 1)
            edge = jnp.concatenate([edge, edge], axis=1)
            return jnp.where(x_at == B - 1, edge, roll(state[c], -B, 1))
        edge = roll(x_before, -c * B, 1)
        edge = jnp.concatenate([edge, edge], axis=1)
        return jnp.where(x_at == 0, edge, roll(state[c], B, 1))

    def y_neighbour(c, up):
        if up:
            return jnp.where(y_at == B - 1, roll(state[c], B - 1, 1), roll(state[c], -1, 1))
        return jnp.where(y_at == 0, roll(state[c], 1 - B, 1), roll(state[c], 1, 1))

    def offsets_in(j):
        return z_at - z0[j], x_at - x0[j], y_at - y0[j]

    def inside(offset):
        return (offset >= 2) & (offset < 6)

    change = None
    correction = [jnp.zeros(big, jnp.float32)] * 5
    for dim, (neighbour, member) in enumerate(
        ((z_neighbour, 3), (x_neighbour, 1), (y_neighbour, 2))
    ):
        low = [neighbour(c, False) for c in range(5)]
        up = [neighbour(c, True) for c in range(5)]
        flux_low = face_flux(low, cell_terms(low), state, terms, member)
        flux_high = face_flux(state, terms, up, cell_terms(up), member)
        below, above = None, None
        for j in range(2):
            off = offsets_in(j)
            others = [inside(off[other]) for other in range(3) if other != dim]
            shared = others[0] & others[1]
            is_below = shared & (off[dim] == 1)
            is_above = shared & (off[dim] == 6)
            below = is_below if below is None else below | is_below
            above = is_above if above is None else above | is_above
        difference = [flux_high[c] - flux_low[c] for c in range(5)]
        change = difference if change is None else [change[c] + difference[c] for c in range(5)]
        correction = [
            jnp.where(below, flux_high[c], jnp.where(above, -flux_low[c], correction[c]))
            for c in range(5)
        ]
    for c in range(5):
        stepped = state[c] - RATIO * change[c]
        half_ref[c] = 0.5 * (state[c] + stepped)
        out_ref[c] = stepped + RATIO * correction[c]

    small = (8, 128)
    row, lane = iota(small, 0), iota(small, 1)
    wide_row = iota((8, ROW), 0)
    half = lane < 64
    even_row = (row & 1) == 0
    box_at, b_at, e_at = lane >> 6, (lane >> 3) & 7, lane & 7
    block_x, block_box, block_y = lane >> 4, (lane >> 3) & 1, lane & 7

    def swap(value):
        return roll(value, 64, 1)

    fine = []
    for c in range(5):
        pick = (c % 2) * 4 + (row >> 1)
        rows = pl.ds((c // 2) * 8, 8)
        first = take(boxes_ref[0, rows, :], pick, 0)
        second = take(boxes_ref[1, rows, :], pick, 0)
        fine.append(
            jnp.where(
                half,
                jnp.where(even_row, first, swap(first)),
                jnp.where(even_row, swap(second), second),
            )
        )

    def block(ref, c):
        parts = []
        for j in range(2):
            rows = jnp.where(wide_row >= z0[j], ref[c, :8, :], ref[c, 8:, :])
            window = jnp.where(lane >= shifts[j], rows[:, :128], rows[:, 128:])
            window = pltpu.roll(window, (8 - z0[j]) & 7, 0)
            parts.append(pltpu.roll(window, (256 - shifts[j] + 8 * j) & 127, 1))
        return jnp.where(block_box == 0, parts[0], parts[1])

    def sign(flag):
        return jnp.where(flag, 0.25, -0.25).astype(jnp.float32)

    towards_z, towards_x, towards_y = sign(row < 4), sign(block_x < 4), sign(block_y < 4)
    child_z, child_x, child_y = (
        sign((row & 1) == 1),
        sign((b_at & 1) == 1),
        sign((e_at & 1) == 1),
    )
    mid_x, mid_y = (2 + (b_at >> 1)) * B, 2 + (e_at >> 1)
    end_x, end_y = jnp.where(b_at < 4, 1, 6) * B, jnp.where(e_at < 4, 1, 6)
    lanes_z = mid_x + box_at * 8 + mid_y
    lanes_x = end_x + box_at * 8 + mid_y
    lanes_y = mid_x + box_at * 8 + end_y
    rows_end = jnp.where(row < 4, 1, 6)
    rows_mid = 2 + (row >> 1)

    def ghosts(ref):
        ghost_z, ghost_x, ghost_y = [], [], []
        for c in range(5):
            field = block(ref, c)

            def slope(axis, step):
                lower = field - roll(field, step, axis)
                return minmod(lower, roll(lower, -step, axis))

            slope_z, slope_x, slope_y = slope(0, 1), slope(1, B), slope(1, 1)
            value = take(field + towards_z * slope_z, lanes_z, 1)
            value = value + child_x * take(slope_x, lanes_z, 1) + child_y * take(slope_y, lanes_z, 1)
            ghost_z.append(take(value, rows_end, 0))
            value = take(field + towards_x * slope_x, lanes_x, 1)
            value = value + child_y * take(slope_y, lanes_x, 1)
            ghost_x.append(
                take(value, rows_mid, 0) + child_z * take(take(slope_z, lanes_x, 1), rows_mid, 0)
            )
            value = take(field + towards_y * slope_y, lanes_y, 1)
            value = value + child_x * take(slope_x, lanes_y, 1)
            ghost_y.append(
                take(value, rows_mid, 0) + child_z * take(take(slope_z, lanes_y, 1), rows_mid, 0)
            )
        return ghost_z, ghost_x, ghost_y

    directions = ((0, 1, row, 3), (1, 8, b_at, 1), (1, 1, e_at, 2))
    sums = [None, None, None]
    for ref in (coarse_ref, half_ref):
        ghost_sets = ghosts(ref)
        terms = cell_terms(fine)
        change = None
        for dim, (axis, step, at, member) in enumerate(directions):
            ghost = ghost_sets[dim]
            low = [jnp.where(at == 0, ghost[c], roll(fine[c], step, axis)) for c in range(5)]
            up = [jnp.where(at == 7, ghost[c], roll(fine[c], -step, axis)) for c in range(5)]
            flux_low = face_flux(low, cell_terms(low), fine, terms, member)
            flux_high = face_flux(fine, terms, up, cell_terms(up), member)
            difference = [flux_high[c] - flux_low[c] for c in range(5)]
            change = difference if change is None else [change[c] + difference[c] for c in range(5)]
            edge = [jnp.where(at < 4, flux_low[c], flux_high[c]) for c in range(5)]
            sums[dim] = edge if sums[dim] is None else [sums[dim][c] + edge[c] for c in range(5)]
        fine = [fine[c] - RATIO * change[c] for c in range(5)]

    back = [[], []]
    for c in range(5):
        swapped = swap(fine[c])
        pick = (row & 3) * 2
        for j, (on_even, on_odd) in enumerate(((fine[c], swapped), (swapped, fine[c]))):
            joined = jnp.where(even_row, on_even, on_odd)
            joined = jnp.where(half, joined, roll(joined, -1, 0))
            back[j].append(take(joined, pick, 0))
    for j in range(2):
        tag = (owner_ref[0, j, 0] * 8 + owner_ref[0, j, 1]).astype(jnp.float32)
        back[j].append(jnp.full(small, tag, jnp.float32))
        for pair in range(3):
            result_ref[j, pair * 8 : pair * 8 + 8, :] = jnp.where(
                row < 4, back[j][2 * pair], back[j][2 * pair + 1]
            )

    near_x, near_y = (block_x - 2) * 16, (block_y - 2) * 2
    far_x, far_y = jnp.where(block_x < 4, 0, 56), jnp.where(block_y < 4, 0, 7)
    back_z = (block_box * 64 + near_x + near_y) & 127
    back_x = (block_box * 64 + far_x + near_y) & 127
    back_y = (block_box * 64 + near_x + far_y) & 127
    back_mid = ((row - 2) * 2) & 7
    back_end = jnp.where(row < 4, 0, 7)
    factor_z = jnp.where(row < 4, -0.125 * RATIO, 0.125 * RATIO).astype(jnp.float32)
    factor_x = jnp.where(block_x < 4, -0.125 * RATIO, 0.125 * RATIO).astype(jnp.float32)
    factor_y = jnp.where(block_y < 4, -0.125 * RATIO, 0.125 * RATIO).astype(jnp.float32)
    on_x = (block_x == 1) | (block_x == 6)
    on_y = (block_y == 1) | (block_y == 6)
    on_z = (row == 1) | (row == 6)

    def add_e(value):
        return value + roll(value, -1, 1)

    def add_b(value):
        return value + roll(value, -8, 1)

    def add_a(value):
        return value + roll(value, -1, 0)

    covered, beside = [], []
    for j in range(2):
        off = offsets_in(j)
        within = [inside(offset) for offset in off]
        at_face = [(offset == 1) | (offset == 6) for offset in off]
        covered.append(within[0] & within[1] & within[2])
        beside.append(
            (at_face[0] & within[1] & within[2])
            | (within[0] & at_face[1] & within[2])
            | (within[0] & within[1] & at_face[2])
        )
    for c in range(5):
        from_z = take(add_b(add_e(sums[0][c])), back_z, 1)
        from_x = take(add_a(add_e(sums[1][c])), back_x, 1)
        from_y = take(add_a(add_b(sums[2][c])), back_y, 1)
        average = take(add_a(add_b(add_e(fine[c]))), back_z, 1)
        mixed = jnp.where(
            on_x, factor_x * from_x, jnp.where(on_y, factor_y * from_y, 0.125 * average)
        )
        placed = jnp.where(on_z, factor_z * take(from_z, back_end, 0), take(mixed, back_mid, 0))
        value = out_ref[c]
        for j in range(2):
            moved = pltpu.roll(placed, (shifts[j] + 128 - 8 * j) & 127, 1)
            moved = pltpu.roll(moved, z0[j] & 7, 0)
            moved = jnp.concatenate([moved, moved], axis=1)
            moved = jnp.concatenate([moved, moved], axis=0)
            value = jnp.where(covered[j], moved, jnp.where(beside[j], value + moved, value))
        out_ref[c] = value


def unpack_kernel(*refs):
    sources, out_ref = refs[:SPAN], refs[SPAN]
    row = iota((8, 128), 0).astype(jnp.float32)
    matches = [
        [sources[k][j, 20:21, :] == row + 8.0 * k for j in range(2)] for k in range(SPAN)
    ]
    for c in range(5):
        for tile in range(4):
            at = c * 4 + tile
            value = jnp.zeros((8, 128), jnp.float32)
            for k in range(SPAN):
                for j in range(2):
                    value = jnp.where(matches[k][j], sources[k][j, at : at + 1, :], value)
            out_ref[c, :, tile * 128 : (tile + 1) * 128] = value[:CAP]


def moved_along(value, axis, steps):
    count = lax.axis_size(axis)
    return lax.ppermute(value, axis, [(i, (i + steps) % count) for i in range(count)])


def full(space):
    return pl.BlockSpec(memory_space=space)


def body(coarse_state, fine_state, fine_anchor, fine_owner):
    def like(*shape):
        return jax.ShapeDtypeStruct(shape, jnp.float32)

    fine_by_comp = jnp.swapaxes(fine_state, 0, 1)
    slots, edges = pl.pallas_call(
        pack_kernel,
        out_shape=(like(CAP * SLOT_ROWS, 128), like(2, B, 128)),
        in_specs=[full(VMEM)] * 2,
        out_specs=[full(VMEM)] * 2,
        name="pack",
    )(coarse_state, fine_by_comp)
    slots = slots.reshape(CAP, SLOT_ROWS, 128)
    devs = lax.axis_size("dev")
    pair = lax.ppermute(edges, "dev", [(d, d ^ 1) for d in range(devs)])
    relay = lax.ppermute(pair, "dev", [(d, (d + 2 - 4 * (d % 2)) % devs) for d in range(devs)])
    fine_parts = [slots] + [moved_along(slots, "node", -k) for k in range(1, SPAN)]
    z_before = moved_along(coarse_state, "node", 1)
    coarse_out, result = pl.pallas_call(
        step_kernel,
        out_shape=(like(5, B, ROW), like(2, SLOT_ROWS, 128)),
        in_specs=[full(SMEM)] * 2 + [full(VMEM)] * 8,
        out_specs=[full(VMEM)] * 2,
        scratch_shapes=[VMEM((5, B, ROW), jnp.float32), VMEM((2, SLOT_ROWS, 128), jnp.float32)],
        name="step",
    )(fine_anchor, fine_owner, coarse_state, *fine_parts, pair, relay, z_before)
    results = [result] + [moved_along(result, "node", k) for k in range(1, SPAN)]
    fine_out = pl.pallas_call(
        unpack_kernel,
        out_shape=like(5, CAP, 512),
        in_specs=[full(VMEM)] * SPAN,
        out_specs=full(VMEM),
        name="unpack",
    )(*results)
    return coarse_out, jnp.swapaxes(fine_out, 0, 1)


def solution(mesh):
    placed = (
        P(None, "node", "dev"),
        P(("node", "dev"), None, None),
        P(("node", "dev"), None, None),
        P(("node", "dev"), None, None),
    )
    return jax.shard_map(
        body,
        mesh=mesh,
        in_specs=placed,
        out_specs=(P(None, "node", "dev"), P(("node", "dev"), None, None)),
        check_vma=False,
    )
```

```python
import functools

import jax
import jax.numpy as jnp
from jax import lax
from jax.experimental import pallas as pl
from jax.experimental.pallas import tpu as pltpu
from jax.sharding import PartitionSpec as P

B = 16
ROW = B * B
CAP = 6
SPAN = 4
SLOT_ROWS = 24
GAMMA = 1.4
RATIO = 0.06
VMEM = pltpu.VMEM
SMEM = pltpu.SMEM


def iota(shape, dim):
    return lax.broadcasted_iota(jnp.int32, shape, dim)


def roll(value, shift, axis):
    size = value.shape[axis]
    return pltpu.roll(value, shift % size, axis)


def take(value, index, axis):
    return jnp.take_along_axis(value, index, axis=axis, mode="promise_in_bounds")


def pack_kernel(coarse_ref, fine_ref, slots_ref, later_ref, edges_ref, z_high_ref):
    lane = iota((B, 128), 1)
    x_low = jnp.zeros((B, 128), jnp.float32)
    x_high = jnp.zeros((B, 128), jnp.float32)
    for c in range(5):
        here = (lane >= c * B) & (lane < (c + 1) * B)
        x_low = jnp.where(here, roll(coarse_ref[c, :, :128], c * B, 1), x_low)
        x_high = jnp.where(here, roll(coarse_ref[c, :, 128:], (c + 1) * B, 1), x_high)
        z_high_ref[c : c + 1, :] = coarse_ref[c, B - 1 : B, :]
    edges_ref[0] = x_low
    edges_ref[1] = x_high
    for slot in range(CAP):
        for c in range(5):
            for tile in range(4):
                at = slot * SLOT_ROWS + c * 4 + tile
                slots_ref[at : at + 1, :] = fine_ref[
                    c, slot : slot + 1, tile * 128 : (tile + 1) * 128
                ]
        at = slot * SLOT_ROWS + 20
        slots_ref[at : at + 4, :] = jnp.zeros((4, 128), jnp.float32)
        if slot < 5:
            slots_ref[at : at + 1, :] = coarse_ref[slot, 0:1, :128]
            slots_ref[at + 1 : at + 2, :] = coarse_ref[slot, 0:1, 128:]
    later_ref[...] = slots_ref[...]


def order_kernel(*refs):
    del refs


def cell_terms(state):
    inverse = 1.0 / state[0]
    squares = state[1] * state[1] + state[2] * state[2] + state[3] * state[3]
    pressure = (GAMMA - 1.0) * (state[4] - 0.5 * squares * inverse)
    sound = jnp.sqrt(GAMMA * pressure * inverse)
    return inverse, pressure, sound


def face_flux(low, low_terms, up, up_terms, member):
    def side(state, terms):
        inverse, pressure, sound = terms
        velocity = state[member] * inverse
        flux = [entry * velocity for entry in state]
        flux[member] = flux[member] + pressure
        flux[4] = flux[4] + pressure * velocity
        return flux, jnp.abs(velocity) + sound

    flux_low, speed_low = side(low, low_terms)
    flux_up, speed_up = side(up, up_terms)
    half_speed = 0.5 * jnp.maximum(speed_low, speed_up)
    return [
        0.5 * (flux_low[c] + flux_up[c]) - half_speed * (up[c] - low[c]) for c in range(5)
    ]


def minmod(lower_diff, upper_diff):
    smaller = jnp.where(jnp.abs(lower_diff) < jnp.abs(upper_diff), lower_diff, upper_diff)
    return jnp.where(lower_diff * upper_diff > 0.0, smaller, 0.0)


def step_kernel(
    anchor_ref,
    owner_ref,
    coarse_ref,
    own_ref,
    one_ref,
    two_ref,
    three_ref,
    pair_ref,
    relay_ref,
    z_before_ref,
    out_ref,
    result_ref,
    half_ref,
    boxes_ref,
):
    z0 = [anchor_ref[0, j, 0] - 2 for j in range(2)]
    x0 = [anchor_ref[0, j, 1] - 2 for j in range(2)]
    y0 = [anchor_ref[0, j, 2] - 2 for j in range(2)]
    shifts = [x0[j] * B + y0[j] for j in range(2)]

    for j in range(2):
        for k, source in enumerate((own_ref, one_ref, two_ref, three_ref)):

            @pl.when(owner_ref[0, j, 0] == k)
            def _(j=j, source=source):
                boxes_ref[j] = source[owner_ref[0, j, 1]]

    odd = lax.rem(lax.axis_index("dev"), 2)
    from_relay = relay_ref[1 - odd]
    x_before = jnp.where(odd == 1, pair_ref[1], from_relay)
    x_after = jnp.where(odd == 1, from_relay, pair_ref[0])

    state = [coarse_ref[c] for c in range(5)]
    terms = cell_terms(state)
    big = (B, ROW)
    z_at, lane = iota(big, 0), iota(big, 1)
    x_at, y_at = lane >> 4, lane & (B - 1)

    def z_neighbour(c, up):
        if up:
            edge = jnp.concatenate([one_ref[c, 20:21, :], one_ref[c, 21:22, :]], axis=1)
            return jnp.where(z_at == B - 1, edge, roll(state[c], -1, 0))
        return jnp.where(z_at == 0, z_before_ref[c : c + 1, :], roll(state[c], 1, 0))

    def x_neighbour(c, up):
        if up:
            edge = roll(x_after, -(c + 1) * B, 1)
            edge = jnp.concatenate([edge, edge], axis=1)
            return jnp.where(x_at == B - 1, edge, roll(state[c], -B, 1))
        edge = roll(x_before, -c * B, 1)
        edge = jnp.concatenate([edge, edge], axis=1)
        return jnp.where(x_at == 0, edge, roll(state[c], B, 1))

    def y_neighbour(c, up):
        if up:
            return jnp.where(y_at == B - 1, roll(state[c], B - 1, 1), roll(state[c], -1, 1))
        return jnp.where(y_at == 0, roll(state[c], 1 - B, 1), roll(state[c], 1, 1))

    def offsets_in(j):
        return z_at - z0[j], x_at - x0[j], y_at - y0[j]

    def inside(offset):
        return (offset >= 2) & (offset < 6)

    change = None
    correction = [jnp.zeros(big, jnp.float32)] * 5
    for dim, (neighbour, member) in enumerate(
        ((z_neighbour, 3), (x_neighbour, 1), (y_neighbour, 2))
    ):
        low = [neighbour(c, False) for c in range(5)]
        up = [neighbour(c, True) for c in range(5)]
        flux_low = face_flux(low, cell_terms(low), state, terms, member)
        flux_high = face_flux(state, terms, up, cell_terms(up), member)
        below, above = None, None
        for j in range(2):
            off = offsets_in(j)
            others = [inside(off[other]) for other in range(3) if other != dim]
            shared = others[0] & others[1]
            is_below = shared & (off[dim] == 1)
            is_above = shared & (off[dim] == 6)
            below = is_below if below is None else below | is_below
            above = is_above if above is None else above | is_above
        difference = [flux_high[c] - flux_low[c] for c in range(5)]
        change = difference if change is None else [change[c] + difference[c] for c in range(5)]
        correction = [
            jnp.where(below, flux_high[c], jnp.where(above, -flux_low[c], correction[c]))
            for c in range(5)
        ]
    for c in range(5):
        stepped = state[c] - RATIO * change[c]
        half_ref[c] = 0.5 * (state[c] + stepped)
        out_ref[c] = stepped + RATIO * correction[c]

    small = (8, 128)
    row, lane = iota(small, 0), iota(small, 1)
    wide_row = iota((8, ROW), 0)
    half = lane < 64
    even_row = (row & 1) == 0
    box_at, b_at, e_at = lane >> 6, (lane >> 3) & 7, lane & 7
    block_x, block_box, block_y = lane >> 4, (lane >> 3) & 1, lane & 7

    def swap(value):
        return roll(value, 64, 1)

    fine = []
    for c in range(5):
        pick = (c % 2) * 4 + (row >> 1)
        rows = pl.ds((c // 2) * 8, 8)
        first = take(boxes_ref[0, rows, :], pick, 0)
        second = take(boxes_ref[1, rows, :], pick, 0)
        fine.append(
            jnp.where(
                half,
                jnp.where(even_row, first, swap(first)),
                jnp.where(even_row, swap(second), second),
            )
        )

    def block(ref, c):
        parts = []
        for j in range(2):
            rows = jnp.where(wide_row >= z0[j], ref[c, :8, :], ref[c, 8:, :])
            window = jnp.where(lane >= shifts[j], rows[:, :128], rows[:, 128:])
            window = pltpu.roll(window, (8 - z0[j]) & 7, 0)
            parts.append(pltpu.roll(window, (256 - shifts[j] + 8 * j) & 127, 1))
        return jnp.where(block_box == 0, parts[0], parts[1])

    def sign(flag):
        return jnp.where(flag, 0.25, -0.25).astype(jnp.float32)

    towards_z, towards_x, towards_y = sign(row < 4), sign(block_x < 4), sign(block_y < 4)
    child_z, child_x, child_y = (
        sign((row & 1) == 1),
        sign((b_at & 1) == 1),
        sign((e_at & 1) == 1),
    )
    mid_x, mid_y = (2 + (b_at >> 1)) * B, 2 + (e_at >> 1)
    end_x, end_y = jnp.where(b_at < 4, 1, 6) * B, jnp.where(e_at < 4, 1, 6)
    lanes_z = mid_x + box_at * 8 + mid_y
    lanes_x = end_x + box_at * 8 + mid_y
    lanes_y = mid_x + box_at * 8 + end_y
    rows_end = jnp.where(row < 4, 1, 6)
    rows_mid = 2 + (row >> 1)

    def ghosts(ref):
        ghost_z, ghost_x, ghost_y = [], [], []
        for c in range(5):
            field = block(ref, c)

            def slope(axis, step):
                lower = field - roll(field, step, axis)
                return minmod(lower, roll(lower, -step, axis))

            slope_z, slope_x, slope_y = slope(0, 1), slope(1, B), slope(1, 1)
            value = take(field + towards_z * slope_z, lanes_z, 1)
            value = value + child_x * take(slope_x, lanes_z, 1) + child_y * take(slope_y, lanes_z, 1)
            ghost_z.append(take(value, rows_end, 0))
            value = take(field + towards_x * slope_x, lanes_x, 1)
            value = value + child_y * take(slope_y, lanes_x, 1)
            ghost_x.append(
                take(value, rows_mid, 0) + child_z * take(take(slope_z, lanes_x, 1), rows_mid, 0)
            )
            value = take(field + towards_y * slope_y, lanes_y, 1)
            value = value + child_x * take(slope_x, lanes_y, 1)
            ghost_y.append(
                take(value, rows_mid, 0) + child_z * take(take(slope_z, lanes_y, 1), rows_mid, 0)
            )
        return ghost_z, ghost_x, ghost_y

    directions = ((0, 1, row, 3), (1, 8, b_at, 1), (1, 1, e_at, 2))
    sums = [None, None, None]
    for ref in (coarse_ref, half_ref):
        ghost_sets = ghosts(ref)
        terms = cell_terms(fine)
        change = None
        for dim, (axis, step, at, member) in enumerate(directions):
            ghost = ghost_sets[dim]
            low = [jnp.where(at == 0, ghost[c], roll(fine[c], step, axis)) for c in range(5)]
            up = [jnp.where(at == 7, ghost[c], roll(fine[c], -step, axis)) for c in range(5)]
            flux_low = face_flux(low, cell_terms(low), fine, terms, member)
            flux_high = face_flux(fine, terms, up, cell_terms(up), member)
            difference = [flux_high[c] - flux_low[c] for c in range(5)]
            change = difference if change is None else [change[c] + difference[c] for c in range(5)]
            edge = [jnp.where(at < 4, flux_low[c], flux_high[c]) for c in range(5)]
            sums[dim] = edge if sums[dim] is None else [sums[dim][c] + edge[c] for c in range(5)]
        fine = [fine[c] - RATIO * change[c] for c in range(5)]

    back = [[], []]
    for c in range(5):
        swapped = swap(fine[c])
        pick = (row & 3) * 2
        for j, (on_even, on_odd) in enumerate(((fine[c], swapped), (swapped, fine[c]))):
            joined = jnp.where(even_row, on_even, on_odd)
            joined = jnp.where(half, joined, roll(joined, -1, 0))
            back[j].append(take(joined, pick, 0))
    for j in range(2):
        tag = (owner_ref[0, j, 0] * 8 + owner_ref[0, j, 1]).astype(jnp.float32)
        back[j].append(jnp.full(small, tag, jnp.float32))
        for pair in range(3):
            result_ref[j, pair * 8 : pair * 8 + 8, :] = jnp.where(
                row < 4, back[j][2 * pair], back[j][2 * pair + 1]
            )

    near_x, near_y = (block_x - 2) * 16, (block_y - 2) * 2
    far_x, far_y = jnp.where(block_x < 4, 0, 56), jnp.where(block_y < 4, 0, 7)
    back_z = (block_box * 64 + near_x + near_y) & 127
    back_x = (block_box * 64 + far_x + near_y) & 127
    back_y = (block_box * 64 + near_x + far_y) & 127
    back_mid = ((row - 2) * 2) & 7
    back_end = jnp.where(row < 4, 0, 7)
    factor_z = jnp.where(row < 4, -0.125 * RATIO, 0.125 * RATIO).astype(jnp.float32)
    factor_x = jnp.where(block_x < 4, -0.125 * RATIO, 0.125 * RATIO).astype(jnp.float32)
    factor_y = jnp.where(block_y < 4, -0.125 * RATIO, 0.125 * RATIO).astype(jnp.float32)
    on_x = (block_x == 1) | (block_x == 6)
    on_y = (block_y == 1) | (block_y == 6)
    on_z = (row == 1) | (row == 6)

    def add_e(value):
        return value + roll(value, -1, 1)

    def add_b(value):
        return value + roll(value, -8, 1)

    def add_a(value):
        return value + roll(value, -1, 0)

    covered, beside = [], []
    for j in range(2):
        off = offsets_in(j)
        within = [inside(offset) for offset in off]
        at_face = [(offset == 1) | (offset == 6) for offset in off]
        covered.append(within[0] & within[1] & within[2])
        beside.append(
            (at_face[0] & within[1] & within[2])
            | (within[0] & at_face[1] & within[2])
            | (within[0] & within[1] & at_face[2])
        )
    for c in range(5):
        from_z = take(add_b(add_e(sums[0][c])), back_z, 1)
        from_x = take(add_a(add_e(sums[1][c])), back_x, 1)
        from_y = take(add_a(add_b(sums[2][c])), back_y, 1)
        average = take(add_a(add_b(add_e(fine[c]))), back_z, 1)
        mixed = jnp.where(
            on_x, factor_x * from_x, jnp.where(on_y, factor_y * from_y, 0.125 * average)
        )
        placed = jnp.where(on_z, factor_z * take(from_z, back_end, 0), take(mixed, back_mid, 0))
        value = out_ref[c]
        for j in range(2):
            moved = pltpu.roll(placed, (shifts[j] + 128 - 8 * j) & 127, 1)
            moved = pltpu.roll(moved, z0[j] & 7, 0)
            moved = jnp.concatenate([moved, moved], axis=1)
            moved = jnp.concatenate([moved, moved], axis=0)
            value = jnp.where(covered[j], moved, jnp.where(beside[j], value + moved, value))
        out_ref[c] = value


def unpack_kernel(*refs):
    sources, out_ref = refs[:SPAN], refs[SPAN]
    row = iota((8, 128), 0).astype(jnp.float32)
    matches = [
        [sources[k][j, 20:21, :] == row + 8.0 * k for j in range(2)] for k in range(SPAN)
    ]
    for c in range(5):
        for tile in range(4):
            at = c * 4 + tile
            value = jnp.zeros((8, 128), jnp.float32)
            for k in range(SPAN):
                for j in range(2):
                    value = jnp.where(matches[k][j], sources[k][j, at : at + 1, :], value)
            out_ref[c, :, tile * 128 : (tile + 1) * 128] = value[:CAP]


def moved_along(value, axis, steps):
    count = lax.axis_size(axis)
    return lax.ppermute(value, axis, [(i, (i + steps) % count) for i in range(count)])


def full(space):
    return pl.BlockSpec(memory_space=space)


def in_order(*values):
    return pl.pallas_call(
        order_kernel,
        out_shape=tuple(jax.ShapeDtypeStruct(value.shape, value.dtype) for value in values),
        in_specs=[full(pl.ANY)] * len(values),
        out_specs=tuple([full(pl.ANY)] * len(values)),
        input_output_aliases={i: i for i in range(len(values))},
        cost_estimate=pl.CostEstimate(flops=10**9, bytes_accessed=10**9, transcendentals=0),
        name="order",
    )(*values)


def body(coarse_state, fine_state, fine_anchor, fine_owner):
    def like(*shape):
        return jax.ShapeDtypeStruct(shape, jnp.float32)

    fine_by_comp = jnp.swapaxes(fine_state, 0, 1)
    slots, later, edges, z_high = pl.pallas_call(
        pack_kernel,
        out_shape=(
            like(CAP * SLOT_ROWS, 128),
            like(CAP * SLOT_ROWS, 128),
            like(2, B, 128),
            like(5, ROW),
        ),
        in_specs=[full(VMEM)] * 2,
        out_specs=[full(VMEM)] * 4,
        name="pack",
    )(coarse_state, fine_by_comp)
    slots = slots.reshape(CAP, SLOT_ROWS, 128)
    devs = lax.axis_size("dev")
    pair = lax.ppermute(edges, "dev", [(d, d ^ 1) for d in range(devs)])
    z_before = moved_along(z_high, "node", 1)
    third = moved_along(slots, "node", -3)
    second = moved_along(slots, "node", -2)
    later, pair, z_before = in_order(later, pair, z_before)
    later = later.reshape(CAP, SLOT_ROWS, 128)
    relay = lax.ppermute(pair, "dev", [(d, (d + 2 - 4 * (d % 2)) % devs) for d in range(devs)])
    relay, second, third = in_order(relay, second, third)
    fine_parts = [slots, moved_along(later, "node", -1), second, third]
    coarse_out, result = pl.pallas_call(
        step_kernel,
        out_shape=(like(5, B, ROW), like(2, SLOT_ROWS, 128)),
        in_specs=[full(SMEM)] * 2 + [full(VMEM)] * 8,
        out_specs=[full(VMEM)] * 2,
        scratch_shapes=[VMEM((5, B, ROW), jnp.float32), VMEM((2, SLOT_ROWS, 128), jnp.float32)],
        name="step",
    )(fine_anchor, fine_owner, coarse_state, *fine_parts, pair, relay, z_before)
    results = [result] + [moved_along(result, "node", k) for k in range(1, SPAN)]
    fine_out = pl.pallas_call(
        unpack_kernel,
        out_shape=like(5, CAP, 512),
        in_specs=[full(VMEM)] * SPAN,
        out_specs=full(VMEM),
        name="unpack",
    )(*results)
    return coarse_out, jnp.swapaxes(fine_out, 0, 1)


def solution(mesh):
    placed = (
        P(None, "node", "dev"),
        P(("node", "dev"), None, None),
        P(("node", "dev"), None, None),
        P(("node", "dev"), None, None),
    )
    return jax.shard_map(
        body,
        mesh=mesh,
        in_specs=placed,
        out_specs=(P(None, "node", "dev"), P(("node", "dev"), None, None)),
        check_vma=False,
    )
```

```python
import functools

import jax
import jax.numpy as jnp
from jax import lax
from jax.experimental import pallas as pl
from jax.experimental.pallas import tpu as pltpu
from jax.sharding import PartitionSpec as P

B = 16
ROW = B * B
CAP = 6
SPAN = 4
SLOT_ROWS = 24
GAMMA = 1.4
RATIO = 0.06
VMEM = pltpu.VMEM
SMEM = pltpu.SMEM


def iota(shape, dim):
    return lax.broadcasted_iota(jnp.int32, shape, dim)


def roll(value, shift, axis):
    size = value.shape[axis]
    return pltpu.roll(value, shift % size, axis)


def take(value, index, axis):
    return jnp.take_along_axis(value, index, axis=axis, mode="promise_in_bounds")


def pack_kernel(coarse_ref, fine_ref, slots_ref, later_ref, edges_ref, z_high_ref):
    lane = iota((B, 128), 1)
    x_low = jnp.zeros((B, 128), jnp.float32)
    x_high = jnp.zeros((B, 128), jnp.float32)
    for c in range(5):
        here = (lane >= c * B) & (lane < (c + 1) * B)
        x_low = jnp.where(here, roll(coarse_ref[c, :, :128], c * B, 1), x_low)
        x_high = jnp.where(here, roll(coarse_ref[c, :, 128:], (c + 1) * B, 1), x_high)
        z_high_ref[c : c + 1, :] = coarse_ref[c, B - 1 : B, :]
    edges_ref[0] = x_low
    edges_ref[1] = x_high
    for slot in range(CAP):
        for c in range(5):
            for tile in range(4):
                at = slot * SLOT_ROWS + c * 4 + tile
                slots_ref[at : at + 1, :] = fine_ref[
                    c, slot : slot + 1, tile * 128 : (tile + 1) * 128
                ]
        at = slot * SLOT_ROWS + 20
        slots_ref[at : at + 4, :] = jnp.zeros((4, 128), jnp.float32)
        if slot < 5:
            slots_ref[at : at + 1, :] = coarse_ref[slot, 0:1, :128]
            slots_ref[at + 1 : at + 2, :] = coarse_ref[slot, 0:1, 128:]
    later_ref[...] = slots_ref[...]


def order_kernel(*refs):
    del refs


def cell_terms(state):
    inverse = 1.0 / state[0]
    squares = state[1] * state[1] + state[2] * state[2] + state[3] * state[3]
    pressure = (GAMMA - 1.0) * (state[4] - 0.5 * squares * inverse)
    sound = jnp.sqrt(GAMMA * pressure * inverse)
    return inverse, pressure, sound


def face_flux(low, low_terms, up, up_terms, member):
    def side(state, terms):
        inverse, pressure, sound = terms
        velocity = state[member] * inverse
        flux = [entry * velocity for entry in state]
        flux[member] = flux[member] + pressure
        flux[4] = flux[4] + pressure * velocity
        return flux, jnp.abs(velocity) + sound

    flux_low, speed_low = side(low, low_terms)
    flux_up, speed_up = side(up, up_terms)
    half_speed = 0.5 * jnp.maximum(speed_low, speed_up)
    return [
        0.5 * (flux_low[c] + flux_up[c]) - half_speed * (up[c] - low[c]) for c in range(5)
    ]


def minmod(lower_diff, upper_diff):
    smaller = jnp.where(jnp.abs(lower_diff) < jnp.abs(upper_diff), lower_diff, upper_diff)
    return jnp.where(lower_diff * upper_diff > 0.0, smaller, 0.0)


def step_kernel(
    anchor_ref,
    owner_ref,
    coarse_ref,
    own_ref,
    one_ref,
    two_ref,
    three_ref,
    pair_ref,
    relay_ref,
    z_before_ref,
    token_ref,
    out_ref,
    result_ref,
    half_ref,
    boxes_ref,
):
    del token_ref
    z0 = [anchor_ref[0, j, 0] - 2 for j in range(2)]
    x0 = [anchor_ref[0, j, 1] - 2 for j in range(2)]
    y0 = [anchor_ref[0, j, 2] - 2 for j in range(2)]
    shifts = [x0[j] * B + y0[j] for j in range(2)]

    for j in range(2):
        for k, source in enumerate((own_ref, one_ref, two_ref, three_ref)):

            @pl.when(owner_ref[0, j, 0] == k)
            def _(j=j, source=source):
                boxes_ref[j] = source[owner_ref[0, j, 1]]

    odd = lax.rem(lax.axis_index("dev"), 2)
    from_relay = relay_ref[1 - odd]
    x_before = jnp.where(odd == 1, pair_ref[1], from_relay)
    x_after = jnp.where(odd == 1, from_relay, pair_ref[0])

    state = [coarse_ref[c] for c in range(5)]
    terms = cell_terms(state)
    big = (B, ROW)
    z_at, lane = iota(big, 0), iota(big, 1)
    x_at, y_at = lane >> 4, lane & (B - 1)

    def z_neighbour(c, up):
        if up:
            edge = jnp.concatenate([one_ref[c, 20:21, :], one_ref[c, 21:22, :]], axis=1)
            return jnp.where(z_at == B - 1, edge, roll(state[c], -1, 0))
        return jnp.where(z_at == 0, z_before_ref[c : c + 1, :], roll(state[c], 1, 0))

    def x_neighbour(c, up):
        if up:
            edge = roll(x_after, -(c + 1) * B, 1)
            edge = jnp.concatenate([edge, edge], axis=1)
            return jnp.where(x_at == B - 1, edge, roll(state[c], -B, 1))
        edge = roll(x_before, -c * B, 1)
        edge = jnp.concatenate([edge, edge], axis=1)
        return jnp.where(x_at == 0, edge, roll(state[c], B, 1))

    def y_neighbour(c, up):
        if up:
            return jnp.where(y_at == B - 1, roll(state[c], B - 1, 1), roll(state[c], -1, 1))
        return jnp.where(y_at == 0, roll(state[c], 1 - B, 1), roll(state[c], 1, 1))

    def offsets_in(j):
        return z_at - z0[j], x_at - x0[j], y_at - y0[j]

    def inside(offset):
        return (offset >= 2) & (offset < 6)

    change = None
    correction = [jnp.zeros(big, jnp.float32)] * 5
    for dim, (neighbour, member) in enumerate(
        ((z_neighbour, 3), (x_neighbour, 1), (y_neighbour, 2))
    ):
        low = [neighbour(c, False) for c in range(5)]
        up = [neighbour(c, True) for c in range(5)]
        flux_low = face_flux(low, cell_terms(low), state, terms, member)
        flux_high = face_flux(state, terms, up, cell_terms(up), member)
        below, above = None, None
        for j in range(2):
            off = offsets_in(j)
            others = [inside(off[other]) for other in range(3) if other != dim]
            shared = others[0] & others[1]
            is_below = shared & (off[dim] == 1)
            is_above = shared & (off[dim] == 6)
            below = is_below if below is None else below | is_below
            above = is_above if above is None else above | is_above
        difference = [flux_high[c] - flux_low[c] for c in range(5)]
        change = difference if change is None else [change[c] + difference[c] for c in range(5)]
        correction = [
            jnp.where(below, flux_high[c], jnp.where(above, -flux_low[c], correction[c]))
            for c in range(5)
        ]
    for c in range(5):
        stepped = state[c] - RATIO * change[c]
        half_ref[c] = 0.5 * (state[c] + stepped)
        out_ref[c] = stepped + RATIO * correction[c]

    small = (8, 128)
    row, lane = iota(small, 0), iota(small, 1)
    wide_row = iota((8, ROW), 0)
    half = lane < 64
    even_row = (row & 1) == 0
    box_at, b_at, e_at = lane >> 6, (lane >> 3) & 7, lane & 7
    block_x, block_box, block_y = lane >> 4, (lane >> 3) & 1, lane & 7

    def swap(value):
        return roll(value, 64, 1)

    fine = []
    for c in range(5):
        pick = (c % 2) * 4 + (row >> 1)
        rows = pl.ds((c // 2) * 8, 8)
        first = take(boxes_ref[0, rows, :], pick, 0)
        second = take(boxes_ref[1, rows, :], pick, 0)
        fine.append(
            jnp.where(
                half,
                jnp.where(even_row, first, swap(first)),
                jnp.where(even_row, swap(second), second),
            )
        )

    def block(ref, c):
        parts = []
        for j in range(2):
            rows = jnp.where(wide_row >= z0[j], ref[c, :8, :], ref[c, 8:, :])
            window = jnp.where(lane >= shifts[j], rows[:, :128], rows[:, 128:])
            window = pltpu.roll(window, (8 - z0[j]) & 7, 0)
            parts.append(pltpu.roll(window, (256 - shifts[j] + 8 * j) & 127, 1))
        return jnp.where(block_box == 0, parts[0], parts[1])

    def sign(flag):
        return jnp.where(flag, 0.25, -0.25).astype(jnp.float32)

    towards_z, towards_x, towards_y = sign(row < 4), sign(block_x < 4), sign(block_y < 4)
    child_z, child_x, child_y = (
        sign((row & 1) == 1),
        sign((b_at & 1) == 1),
        sign((e_at & 1) == 1),
    )
    mid_x, mid_y = (2 + (b_at >> 1)) * B, 2 + (e_at >> 1)
    end_x, end_y = jnp.where(b_at < 4, 1, 6) * B, jnp.where(e_at < 4, 1, 6)
    lanes_z = mid_x + box_at * 8 + mid_y
    lanes_x = end_x + box_at * 8 + mid_y
    lanes_y = mid_x + box_at * 8 + end_y
    rows_end = jnp.where(row < 4, 1, 6)
    rows_mid = 2 + (row >> 1)

    def ghosts(ref):
        ghost_z, ghost_x, ghost_y = [], [], []
        for c in range(5):
            field = block(ref, c)

            def slope(axis, step):
                lower = field - roll(field, step, axis)
                return minmod(lower, roll(lower, -step, axis))

            slope_z, slope_x, slope_y = slope(0, 1), slope(1, B), slope(1, 1)
            value = take(field + towards_z * slope_z, lanes_z, 1)
            value = value + child_x * take(slope_x, lanes_z, 1) + child_y * take(slope_y, lanes_z, 1)
            ghost_z.append(take(value, rows_end, 0))
            value = take(field + towards_x * slope_x, lanes_x, 1)
            value = value + child_y * take(slope_y, lanes_x, 1)
            ghost_x.append(
                take(value, rows_mid, 0) + child_z * take(take(slope_z, lanes_x, 1), rows_mid, 0)
            )
            value = take(field + towards_y * slope_y, lanes_y, 1)
            value = value + child_x * take(slope_x, lanes_y, 1)
            ghost_y.append(
                take(value, rows_mid, 0) + child_z * take(take(slope_z, lanes_y, 1), rows_mid, 0)
            )
        return ghost_z, ghost_x, ghost_y

    directions = ((0, 1, row, 3), (1, 8, b_at, 1), (1, 1, e_at, 2))
    sums = [None, None, None]
    for ref in (coarse_ref, half_ref):
        ghost_sets = ghosts(ref)
        terms = cell_terms(fine)
        change = None
        for dim, (axis, step, at, member) in enumerate(directions):
            ghost = ghost_sets[dim]
            low = [jnp.where(at == 0, ghost[c], roll(fine[c], step, axis)) for c in range(5)]
            up = [jnp.where(at == 7, ghost[c], roll(fine[c], -step, axis)) for c in range(5)]
            flux_low = face_flux(low, cell_terms(low), fine, terms, member)
            flux_high = face_flux(fine, terms, up, cell_terms(up), member)
            difference = [flux_high[c] - flux_low[c] for c in range(5)]
            change = difference if change is None else [change[c] + difference[c] for c in range(5)]
            edge = [jnp.where(at < 4, flux_low[c], flux_high[c]) for c in range(5)]
            sums[dim] = edge if sums[dim] is None else [sums[dim][c] + edge[c] for c in range(5)]
        fine = [fine[c] - RATIO * change[c] for c in range(5)]

    back = [[], []]
    for c in range(5):
        swapped = swap(fine[c])
        pick = (row & 3) * 2
        for j, (on_even, on_odd) in enumerate(((fine[c], swapped), (swapped, fine[c]))):
            joined = jnp.where(even_row, on_even, on_odd)
            joined = jnp.where(half, joined, roll(joined, -1, 0))
            back[j].append(take(joined, pick, 0))
    for j in range(2):
        tag = (owner_ref[0, j, 0] * 8 + owner_ref[0, j, 1]).astype(jnp.float32)
        back[j].append(jnp.full(small, tag, jnp.float32))
        for pair in range(3):
            result_ref[j, pair * 8 : pair * 8 + 8, :] = jnp.where(
                row < 4, back[j][2 * pair], back[j][2 * pair + 1]
            )

    near_x, near_y = (block_x - 2) * 16, (block_y - 2) * 2
    far_x, far_y = jnp.where(block_x < 4, 0, 56), jnp.where(block_y < 4, 0, 7)
    back_z = (block_box * 64 + near_x + near_y) & 127
    back_x = (block_box * 64 + far_x + near_y) & 127
    back_y = (block_box * 64 + near_x + far_y) & 127
    back_mid = ((row - 2) * 2) & 7
    back_end = jnp.where(row < 4, 0, 7)
    factor_z = jnp.where(row < 4, -0.125 * RATIO, 0.125 * RATIO).astype(jnp.float32)
    factor_x = jnp.where(block_x < 4, -0.125 * RATIO, 0.125 * RATIO).astype(jnp.float32)
    factor_y = jnp.where(block_y < 4, -0.125 * RATIO, 0.125 * RATIO).astype(jnp.float32)
    on_x = (block_x == 1) | (block_x == 6)
    on_y = (block_y == 1) | (block_y == 6)
    on_z = (row == 1) | (row == 6)

    def add_e(value):
        return value + roll(value, -1, 1)

    def add_b(value):
        return value + roll(value, -8, 1)

    def add_a(value):
        return value + roll(value, -1, 0)

    covered, beside = [], []
    for j in range(2):
        off = offsets_in(j)
        within = [inside(offset) for offset in off]
        at_face = [(offset == 1) | (offset == 6) for offset in off]
        covered.append(within[0] & within[1] & within[2])
        beside.append(
            (at_face[0] & within[1] & within[2])
            | (within[0] & at_face[1] & within[2])
            | (within[0] & within[1] & at_face[2])
        )
    for c in range(5):
        from_z = take(add_b(add_e(sums[0][c])), back_z, 1)
        from_x = take(add_a(add_e(sums[1][c])), back_x, 1)
        from_y = take(add_a(add_b(sums[2][c])), back_y, 1)
        average = take(add_a(add_b(add_e(fine[c]))), back_z, 1)
        mixed = jnp.where(
            on_x, factor_x * from_x, jnp.where(on_y, factor_y * from_y, 0.125 * average)
        )
        placed = jnp.where(on_z, factor_z * take(from_z, back_end, 0), take(mixed, back_mid, 0))
        value = out_ref[c]
        for j in range(2):
            moved = pltpu.roll(placed, (shifts[j] + 128 - 8 * j) & 127, 1)
            moved = pltpu.roll(moved, z0[j] & 7, 0)
            moved = jnp.concatenate([moved, moved], axis=1)
            moved = jnp.concatenate([moved, moved], axis=0)
            value = jnp.where(covered[j], moved, jnp.where(beside[j], value + moved, value))
        out_ref[c] = value


def unpack_kernel(*refs):
    sources, out_ref = refs[:SPAN], refs[SPAN]
    row = iota((8, 128), 0).astype(jnp.float32)
    matches = [
        [sources[k][j, 20:21, :] == row + 8.0 * k for j in range(2)] for k in range(SPAN)
    ]
    for c in range(5):
        for tile in range(4):
            at = c * 4 + tile
            value = jnp.zeros((8, 128), jnp.float32)
            for k in range(SPAN):
                for j in range(2):
                    value = jnp.where(matches[k][j], sources[k][j, at : at + 1, :], value)
            out_ref[c, :, tile * 128 : (tile + 1) * 128] = value[:CAP]


def moved_along(value, axis, steps):
    count = lax.axis_size(axis)
    return lax.ppermute(value, axis, [(i, (i + steps) % count) for i in range(count)])


def full(space):
    return pl.BlockSpec(memory_space=space)


def in_order(*values):
    return pl.pallas_call(
        order_kernel,
        out_shape=tuple(jax.ShapeDtypeStruct(value.shape, value.dtype) for value in values),
        in_specs=[full(pl.ANY)] + [full(pltpu.HBM)] * (len(values) - 1),
        out_specs=tuple([full(pl.ANY)] + [full(pltpu.HBM)] * (len(values) - 1)),
        input_output_aliases={i: i for i in range(len(values))},
        cost_estimate=pl.CostEstimate(flops=10**9, bytes_accessed=10**9, transcendentals=0),
        name="order",
    )(*values)


def body(coarse_state, fine_state, fine_anchor, fine_owner):
    def like(*shape):
        return jax.ShapeDtypeStruct(shape, jnp.float32)

    fine_by_comp = jnp.swapaxes(fine_state, 0, 1)
    slots, later, edges, z_high = pl.pallas_call(
        pack_kernel,
        out_shape=(
            like(CAP * SLOT_ROWS, 128),
            like(CAP * SLOT_ROWS, 128),
            like(2, B, 128),
            like(5, ROW),
        ),
        in_specs=[full(VMEM)] * 2,
        out_specs=[full(VMEM)] * 4,
        name="pack",
    )(coarse_state, fine_by_comp)
    slots = slots.reshape(CAP, SLOT_ROWS, 128)
    devs = lax.axis_size("dev")
    pair = lax.ppermute(edges, "dev", [(d, d ^ 1) for d in range(devs)])
    z_before = moved_along(z_high, "node", 1)
    third = moved_along(slots, "node", -3)
    second = moved_along(slots, "node", -2)
    later, pair, z_before = in_order(later, pair, z_before)
    later = later.reshape(CAP, SLOT_ROWS, 128)
    relay = lax.ppermute(pair, "dev", [(d, (d + 2 - 4 * (d % 2)) % devs) for d in range(devs)])
    token = pl.pallas_call(
        order_kernel,
        out_shape=like(8, 128),
        in_specs=[full(pltpu.HBM)] * 3,
        out_specs=full(pltpu.HBM),
        cost_estimate=pl.CostEstimate(flops=10**9, bytes_accessed=10**9, transcendentals=0),
        name="order",
    )(relay, second, third)
    fine_parts = [slots, moved_along(later, "node", -1), second, third]
    coarse_out, result = pl.pallas_call(
        step_kernel,
        out_shape=(like(5, B, ROW), like(2, SLOT_ROWS, 128)),
        in_specs=[full(SMEM)] * 2 + [full(VMEM)] * 8 + [full(pl.ANY)],
        out_specs=[full(VMEM)] * 2,
        scratch_shapes=[VMEM((5, B, ROW), jnp.float32), VMEM((2, SLOT_ROWS, 128), jnp.float32)],
        name="step",
    )(fine_anchor, fine_owner, coarse_state, *fine_parts, pair, relay, z_before, token)
    results = [result] + [moved_along(result, "node", k) for k in range(1, SPAN)]
    fine_out = pl.pallas_call(
        unpack_kernel,
        out_shape=like(5, CAP, 512),
        in_specs=[full(VMEM)] * SPAN,
        out_specs=full(VMEM),
        name="unpack",
    )(*results)
    return coarse_out, jnp.swapaxes(fine_out, 0, 1)


def solution(mesh):
    placed = (
        P(None, "node", "dev"),
        P(("node", "dev"), None, None),
        P(("node", "dev"), None, None),
        P(("node", "dev"), None, None),
    )
    return jax.shard_map(
        body,
        mesh=mesh,
        in_specs=placed,
        out_specs=(P(None, "node", "dev"), P(("node", "dev"), None, None)),
        check_vma=False,
    )
```

```python
import functools

import jax
import jax.numpy as jnp
from jax import lax
from jax.experimental import pallas as pl
from jax.experimental.pallas import tpu as pltpu
from jax.sharding import PartitionSpec as P

B = 16
ROW = B * B
CAP = 6
SPAN = 4
SLOT_ROWS = 24
GAMMA = 1.4
RATIO = 0.06
VMEM = pltpu.VMEM
SMEM = pltpu.SMEM


def iota(shape, dim):
    return lax.broadcasted_iota(jnp.int32, shape, dim)


def roll(value, shift, axis):
    size = value.shape[axis]
    return pltpu.roll(value, shift % size, axis)


def take(value, index, axis):
    return jnp.take_along_axis(value, index, axis=axis, mode="promise_in_bounds")


def pack_kernel(coarse_ref, fine_ref, slots_ref, later_ref, edges_ref, z_high_ref):
    lane = iota((B, 128), 1)
    x_low = jnp.zeros((B, 128), jnp.float32)
    x_high = jnp.zeros((B, 128), jnp.float32)
    for c in range(5):
        here = (lane >= c * B) & (lane < (c + 1) * B)
        x_low = jnp.where(here, roll(coarse_ref[c, :, :128], c * B, 1), x_low)
        x_high = jnp.where(here, roll(coarse_ref[c, :, 128:], (c + 1) * B, 1), x_high)
        z_high_ref[c : c + 1, :] = coarse_ref[c, B - 1 : B, :]
    edges_ref[0] = x_low
    edges_ref[1] = x_high
    for slot in range(CAP):
        for c in range(5):
            for tile in range(4):
                at = slot * SLOT_ROWS + c * 4 + tile
                slots_ref[at : at + 1, :] = fine_ref[
                    c, slot : slot + 1, tile * 128 : (tile + 1) * 128
                ]
        at = slot * SLOT_ROWS + 20
        slots_ref[at : at + 4, :] = jnp.zeros((4, 128), jnp.float32)
        if slot < 5:
            slots_ref[at : at + 1, :] = coarse_ref[slot, 0:1, :128]
            slots_ref[at + 1 : at + 2, :] = coarse_ref[slot, 0:1, 128:]
    later_ref[...] = slots_ref[...]


def order_kernel(*refs):
    del refs


def cell_terms(state):
    inverse = 1.0 / state[0]
    squares = state[1] * state[1] + state[2] * state[2] + state[3] * state[3]
    pressure = (GAMMA - 1.0) * (state[4] - 0.5 * squares * inverse)
    sound = jnp.sqrt(GAMMA * pressure * inverse)
    return inverse, pressure, sound


def face_flux(low, low_terms, up, up_terms, member):
    def side(state, terms):
        inverse, pressure, sound = terms
        velocity = state[member] * inverse
        flux = [entry * velocity for entry in state]
        flux[member] = flux[member] + pressure
        flux[4] = flux[4] + pressure * velocity
        return flux, jnp.abs(velocity) + sound

    flux_low, speed_low = side(low, low_terms)
    flux_up, speed_up = side(up, up_terms)
    half_speed = 0.5 * jnp.maximum(speed_low, speed_up)
    return [
        0.5 * (flux_low[c] + flux_up[c]) - half_speed * (up[c] - low[c]) for c in range(5)
    ]


def minmod(lower_diff, upper_diff):
    smaller = jnp.where(jnp.abs(lower_diff) < jnp.abs(upper_diff), lower_diff, upper_diff)
    return jnp.where(lower_diff * upper_diff > 0.0, smaller, 0.0)


def step_kernel(
    anchor_ref,
    owner_ref,
    coarse_ref,
    own_ref,
    one_ref,
    two_ref,
    three_ref,
    pair_ref,
    relay_ref,
    z_before_ref,
    token_ref,
    out_ref,
    result_ref,
    half_ref,
    boxes_ref,
):
    del token_ref
    z0 = [anchor_ref[0, j, 0] - 2 for j in range(2)]
    x0 = [anchor_ref[0, j, 1] - 2 for j in range(2)]
    y0 = [anchor_ref[0, j, 2] - 2 for j in range(2)]
    shifts = [x0[j] * B + y0[j] for j in range(2)]

    for j in range(2):
        for k, source in enumerate((own_ref, one_ref, two_ref, three_ref)):

            @pl.when(owner_ref[0, j, 0] == k)
            def _(j=j, source=source):
                boxes_ref[j] = source[owner_ref[0, j, 1]]

    odd = lax.rem(lax.axis_index("dev"), 2)
    from_relay = relay_ref[1 - odd]
    x_before = jnp.where(odd == 1, pair_ref[1], from_relay)
    x_after = jnp.where(odd == 1, from_relay, pair_ref[0])

    state = [coarse_ref[c] for c in range(5)]
    terms = cell_terms(state)
    big = (B, ROW)
    z_at, lane = iota(big, 0), iota(big, 1)
    x_at, y_at = lane >> 4, lane & (B - 1)

    def z_neighbour(c, up):
        if up:
            edge = jnp.concatenate([one_ref[c, 20:21, :], one_ref[c, 21:22, :]], axis=1)
            return jnp.where(z_at == B - 1, edge, roll(state[c], -1, 0))
        return jnp.where(z_at == 0, z_before_ref[c : c + 1, :], roll(state[c], 1, 0))

    def x_neighbour(c, up):
        if up:
            edge = roll(x_after, -(c + 1) * B, 1)
            edge = jnp.concatenate([edge, edge], axis=1)
            return jnp.where(x_at == B - 1, edge, roll(state[c], -B, 1))
        edge = roll(x_before, -c * B, 1)
        edge = jnp.concatenate([edge, edge], axis=1)
        return jnp.where(x_at == 0, edge, roll(state[c], B, 1))

    def y_neighbour(c, up):
        if up:
            return jnp.where(y_at == B - 1, roll(state[c], B - 1, 1), roll(state[c], -1, 1))
        return jnp.where(y_at == 0, roll(state[c], 1 - B, 1), roll(state[c], 1, 1))

    def offsets_in(j):
        return z_at - z0[j], x_at - x0[j], y_at - y0[j]

    def inside(offset):
        return (offset >= 2) & (offset < 6)

    change = None
    correction = [jnp.zeros(big, jnp.float32)] * 5
    for dim, (neighbour, member) in enumerate(
        ((z_neighbour, 3), (x_neighbour, 1), (y_neighbour, 2))
    ):
        low = [neighbour(c, False) for c in range(5)]
        up = [neighbour(c, True) for c in range(5)]
        flux_low = face_flux(low, cell_terms(low), state, terms, member)
        flux_high = face_flux(state, terms, up, cell_terms(up), member)
        below, above = None, None
        for j in range(2):
            off = offsets_in(j)
            others = [inside(off[other]) for other in range(3) if other != dim]
            shared = others[0] & others[1]
            is_below = shared & (off[dim] == 1)
            is_above = shared & (off[dim] == 6)
            below = is_below if below is None else below | is_below
            above = is_above if above is None else above | is_above
        difference = [flux_high[c] - flux_low[c] for c in range(5)]
        change = difference if change is None else [change[c] + difference[c] for c in range(5)]
        correction = [
            jnp.where(below, flux_high[c], jnp.where(above, -flux_low[c], correction[c]))
            for c in range(5)
        ]
    for c in range(5):
        stepped = state[c] - RATIO * change[c]
        half_ref[c] = 0.5 * (state[c] + stepped)
        out_ref[c] = stepped + RATIO * correction[c]

    small = (8, 128)
    row, lane = iota(small, 0), iota(small, 1)
    wide_row = iota((8, ROW), 0)
    half = lane < 64
    even_row = (row & 1) == 0
    box_at, b_at, e_at = lane >> 6, (lane >> 3) & 7, lane & 7
    block_x, block_box, block_y = lane >> 4, (lane >> 3) & 1, lane & 7

    def swap(value):
        return roll(value, 64, 1)

    fine = []
    for c in range(5):
        pick = (c % 2) * 4 + (row >> 1)
        rows = pl.ds((c // 2) * 8, 8)
        first = take(boxes_ref[0, rows, :], pick, 0)
        second = take(boxes_ref[1, rows, :], pick, 0)
        fine.append(
            jnp.where(
                half,
                jnp.where(even_row, first, swap(first)),
                jnp.where(even_row, swap(second), second),
            )
        )

    def block(ref, c):
        parts = []
        for j in range(2):
            rows = jnp.where(wide_row >= z0[j], ref[c, :8, :], ref[c, 8:, :])
            window = jnp.where(lane >= shifts[j], rows[:, :128], rows[:, 128:])
            window = pltpu.roll(window, (8 - z0[j]) & 7, 0)
            parts.append(pltpu.roll(window, (256 - shifts[j] + 8 * j) & 127, 1))
        return jnp.where(block_box == 0, parts[0], parts[1])

    def sign(flag):
        return jnp.where(flag, 0.25, -0.25).astype(jnp.float32)

    towards_z, towards_x, towards_y = sign(row < 4), sign(block_x < 4), sign(block_y < 4)
    child_z, child_x, child_y = (
        sign((row & 1) == 1),
        sign((b_at & 1) == 1),
        sign((e_at & 1) == 1),
    )
    mid_x, mid_y = (2 + (b_at >> 1)) * B, 2 + (e_at >> 1)
    end_x, end_y = jnp.where(b_at < 4, 1, 6) * B, jnp.where(e_at < 4, 1, 6)
    lanes_z = mid_x + box_at * 8 + mid_y
    lanes_x = end_x + box_at * 8 + mid_y
    lanes_y = mid_x + box_at * 8 + end_y
    rows_end = jnp.where(row < 4, 1, 6)
    rows_mid = 2 + (row >> 1)

    def ghosts(ref):
        ghost_z, ghost_x, ghost_y = [], [], []
        for c in range(5):
            field = block(ref, c)

            def slope(axis, step):
                lower = field - roll(field, step, axis)
                return minmod(lower, roll(lower, -step, axis))

            slope_z, slope_x, slope_y = slope(0, 1), slope(1, B), slope(1, 1)
            value = take(field + towards_z * slope_z, lanes_z, 1)
            value = value + child_x * take(slope_x, lanes_z, 1) + child_y * take(slope_y, lanes_z, 1)
            ghost_z.append(take(value, rows_end, 0))
            value = take(field + towards_x * slope_x, lanes_x, 1)
            value = value + child_y * take(slope_y, lanes_x, 1)
            ghost_x.append(
                take(value, rows_mid, 0) + child_z * take(take(slope_z, lanes_x, 1), rows_mid, 0)
            )
            value = take(field + towards_y * slope_y, lanes_y, 1)
            value = value + child_x * take(slope_x, lanes_y, 1)
            ghost_y.append(
                take(value, rows_mid, 0) + child_z * take(take(slope_z, lanes_y, 1), rows_mid, 0)
            )
        return ghost_z, ghost_x, ghost_y

    directions = ((0, 1, row, 3), (1, 8, b_at, 1), (1, 1, e_at, 2))
    sums = [None, None, None]
    for ref in (coarse_ref, half_ref):
        ghost_sets = ghosts(ref)
        terms = cell_terms(fine)
        change = None
        for dim, (axis, step, at, member) in enumerate(directions):
            ghost = ghost_sets[dim]
            low = [jnp.where(at == 0, ghost[c], roll(fine[c], step, axis)) for c in range(5)]
            up = [jnp.where(at == 7, ghost[c], roll(fine[c], -step, axis)) for c in range(5)]
            flux_low = face_flux(low, cell_terms(low), fine, terms, member)
            flux_high = face_flux(fine, terms, up, cell_terms(up), member)
            difference = [flux_high[c] - flux_low[c] for c in range(5)]
            change = difference if change is None else [change[c] + difference[c] for c in range(5)]
            edge = [jnp.where(at < 4, flux_low[c], flux_high[c]) for c in range(5)]
            sums[dim] = edge if sums[dim] is None else [sums[dim][c] + edge[c] for c in range(5)]
        fine = [fine[c] - RATIO * change[c] for c in range(5)]

    back = [[], []]
    for c in range(5):
        swapped = swap(fine[c])
        pick = (row & 3) * 2
        for j, (on_even, on_odd) in enumerate(((fine[c], swapped), (swapped, fine[c]))):
            joined = jnp.where(even_row, on_even, on_odd)
            joined = jnp.where(half, joined, roll(joined, -1, 0))
            back[j].append(take(joined, pick, 0))
    for j in range(2):
        tag = (owner_ref[0, j, 0] * 8 + owner_ref[0, j, 1]).astype(jnp.float32)
        back[j].append(jnp.full(small, tag, jnp.float32))
        for pair in range(3):
            result_ref[j, pair * 8 : pair * 8 + 8, :] = jnp.where(
                row < 4, back[j][2 * pair], back[j][2 * pair + 1]
            )

    near_x, near_y = (block_x - 2) * 16, (block_y - 2) * 2
    far_x, far_y = jnp.where(block_x < 4, 0, 56), jnp.where(block_y < 4, 0, 7)
    back_z = (block_box * 64 + near_x + near_y) & 127
    back_x = (block_box * 64 + far_x + near_y) & 127
    back_y = (block_box * 64 + near_x + far_y) & 127
    back_mid = ((row - 2) * 2) & 7
    back_end = jnp.where(row < 4, 0, 7)
    factor_z = jnp.where(row < 4, -0.125 * RATIO, 0.125 * RATIO).astype(jnp.float32)
    factor_x = jnp.where(block_x < 4, -0.125 * RATIO, 0.125 * RATIO).astype(jnp.float32)
    factor_y = jnp.where(block_y < 4, -0.125 * RATIO, 0.125 * RATIO).astype(jnp.float32)
    on_x = (block_x == 1) | (block_x == 6)
    on_y = (block_y == 1) | (block_y == 6)
    on_z = (row == 1) | (row == 6)

    def add_e(value):
        return value + roll(value, -1, 1)

    def add_b(value):
        return value + roll(value, -8, 1)

    def add_a(value):
        return value + roll(value, -1, 0)

    covered, beside = [], []
    for j in range(2):
        off = offsets_in(j)
        within = [inside(offset) for offset in off]
        at_face = [(offset == 1) | (offset == 6) for offset in off]
        covered.append(within[0] & within[1] & within[2])
        beside.append(
            (at_face[0] & within[1] & within[2])
            | (within[0] & at_face[1] & within[2])
            | (within[0] & within[1] & at_face[2])
        )
    for c in range(5):
        from_z = take(add_b(add_e(sums[0][c])), back_z, 1)
        from_x = take(add_a(add_e(sums[1][c])), back_x, 1)
        from_y = take(add_a(add_b(sums[2][c])), back_y, 1)
        average = take(add_a(add_b(add_e(fine[c]))), back_z, 1)
        mixed = jnp.where(
            on_x, factor_x * from_x, jnp.where(on_y, factor_y * from_y, 0.125 * average)
        )
        placed = jnp.where(on_z, factor_z * take(from_z, back_end, 0), take(mixed, back_mid, 0))
        value = out_ref[c]
        for j in range(2):
            moved = pltpu.roll(placed, (shifts[j] + 128 - 8 * j) & 127, 1)
            moved = pltpu.roll(moved, z0[j] & 7, 0)
            moved = jnp.concatenate([moved, moved], axis=1)
            moved = jnp.concatenate([moved, moved], axis=0)
            value = jnp.where(covered[j], moved, jnp.where(beside[j], value + moved, value))
        out_ref[c] = value


def unpack_kernel(*refs):
    sources, out_ref = refs[:SPAN], refs[SPAN]
    row = iota((8, 128), 0).astype(jnp.float32)
    matches = [
        [sources[k][j, 20:21, :] == row + 8.0 * k for j in range(2)] for k in range(SPAN)
    ]
    for c in range(5):
        for tile in range(4):
            at = c * 4 + tile
            value = jnp.zeros((8, 128), jnp.float32)
            for k in range(SPAN):
                for j in range(2):
                    value = jnp.where(matches[k][j], sources[k][j, at : at + 1, :], value)
            out_ref[c, :, tile * 128 : (tile + 1) * 128] = value[:CAP]


def moved_along(value, axis, steps):
    count = lax.axis_size(axis)
    return lax.ppermute(value, axis, [(i, (i + steps) % count) for i in range(count)])


def full(space):
    return pl.BlockSpec(memory_space=space)


def in_order(value, *earlier):
    return pl.pallas_call(
        order_kernel,
        out_shape=jax.ShapeDtypeStruct(value.shape, value.dtype),
        in_specs=[full(pl.ANY)] + [full(pltpu.HBM)] * len(earlier),
        out_specs=full(pl.ANY),
        input_output_aliases={0: 0},
        cost_estimate=pl.CostEstimate(flops=10**9, bytes_accessed=10**9, transcendentals=0),
        name="order",
    )(value, *earlier)


def body(coarse_state, fine_state, fine_anchor, fine_owner):
    def like(*shape):
        return jax.ShapeDtypeStruct(shape, jnp.float32)

    fine_by_comp = jnp.swapaxes(fine_state, 0, 1)
    slots, later, edges, z_high = pl.pallas_call(
        pack_kernel,
        out_shape=(
            like(CAP * SLOT_ROWS, 128),
            like(CAP * SLOT_ROWS, 128),
            like(2, B, 128),
            like(5, ROW),
        ),
        in_specs=[full(VMEM)] * 2,
        out_specs=[full(VMEM)] * 4,
        name="pack",
    )(coarse_state, fine_by_comp)
    slots = slots.reshape(CAP, SLOT_ROWS, 128)
    devs = lax.axis_size("dev")
    pair = lax.ppermute(edges, "dev", [(d, d ^ 1) for d in range(devs)])
    z_before = moved_along(z_high, "node", 1)
    third = moved_along(slots, "node", -3)
    second = moved_along(slots, "node", -2)
    later = in_order(later, pair, z_before)
    later = later.reshape(CAP, SLOT_ROWS, 128)
    relay = lax.ppermute(pair, "dev", [(d, (d + 2 - 4 * (d % 2)) % devs) for d in range(devs)])
    token = pl.pallas_call(
        order_kernel,
        out_shape=like(8, 128),
        in_specs=[full(pltpu.HBM)] * 3,
        out_specs=full(pltpu.HBM),
        cost_estimate=pl.CostEstimate(flops=10**9, bytes_accessed=10**9, transcendentals=0),
        name="order",
    )(relay, second, third)
    fine_parts = [slots, moved_along(later, "node", -1), second, third]
    coarse_out, result = pl.pallas_call(
        step_kernel,
        out_shape=(like(5, B, ROW), like(2, SLOT_ROWS, 128)),
        in_specs=[full(SMEM)] * 2 + [full(VMEM)] * 8 + [full(pl.ANY)],
        out_specs=[full(VMEM)] * 2,
        scratch_shapes=[VMEM((5, B, ROW), jnp.float32), VMEM((2, SLOT_ROWS, 128), jnp.float32)],
        name="step",
    )(fine_anchor, fine_owner, coarse_state, *fine_parts, pair, relay, z_before, token)
    results = [result] + [moved_along(result, "node", k) for k in range(1, SPAN)]
    fine_out = pl.pallas_call(
        unpack_kernel,
        out_shape=like(5, CAP, 512),
        in_specs=[full(VMEM)] * SPAN,
        out_specs=full(VMEM),
        name="unpack",
    )(*results)
    return coarse_out, jnp.swapaxes(fine_out, 0, 1)


def solution(mesh):
    placed = (
        P(None, "node", "dev"),
        P(("node", "dev"), None, None),
        P(("node", "dev"), None, None),
        P(("node", "dev"), None, None),
    )
    return jax.shard_map(
        body,
        mesh=mesh,
        in_specs=placed,
        out_specs=(P(None, "node", "dev"), P(("node", "dev"), None, None)),
        check_vma=False,
    )
```
